256 devices in a mesh: dp: 8 (over x, y_lo), tensor: 32 (over z, y_hi, core).
Axes of the slice: x: 4, y: 4 (y_hi: 2, y_lo: 2; y = y_hi * 2 + y_lo), z: 8, core: 2. Of those that a mesh axis runs over, the one named last changes fastest.
Arguments:
- x_rows: bfloat16 [3072, 4096], P(('dp', 'tensor')), may hold values from -6 to 6
- out_grad: bfloat16 [3072, 4096], P(('dp', 'tensor')), may hold values from -6 to 6
- gate_codes: bfloat16 [4096, 14848], P(None, 'tensor'), may hold values from -4 to 4
- gate_exps: int32 [32, 928], P(None, 'tensor'), may hold values from -8 to -5
- up_codes: bfloat16 [4096, 14848], P(None, 'tensor'), may hold values from -4 to 4
- up_exps: int32 [32, 928], P(None, 'tensor'), may hold values from -8 to -5
- down_codes: bfloat16 [14848, 4096], P('tensor'), may hold values from -4 to 4
- down_exps: int32 [928, 32], P('tensor'), may hold values from -9 to -6
- replay_slot: int32 [3072], P('dp'), may hold values from 0 to 16383
- priorities: float32 [16384], replicated, may hold values from 0.01 to 1
Outputs:
- input_grad: bfloat16 [3072, 4096], P(('dp', 'tensor'))
- gate_grad: bfloat16 [4096, 14848], P('dp', 'tensor')
- up_grad: bfloat16 [4096, 14848], P('dp', 'tensor')
- down_grad: bfloat16 [14848, 4096], P('tensor', 'dp')
The draws below stay inside these ranges and needn't reach their ends.
All inputs are finite; a program needn't handle non-finite values.
Results may differ from the reference program's by a relative error of at most 0.025.
Values may be sent and summed in bfloat16 or wider, within the bound.
No kernel may reach another device: no remote copies, remote signals or barrier semaphores. Data moves between devices by JAX's collectives and lax.ppermute only.
A program may use at most 128 MiB of HBM per device.

```python
import math
import jax
import jax.numpy as jnp
from jax import lax

D = 4096
FF = 14848
TOK_DEV = 384
SLOTS = 16384
BLK_D = 128
BLK_F = 16
TOKENS = 3072


def touch_ends(array, key, low, top_value):
    dims = array.shape
    place = [jax.random.randint(jax.random.fold_in(key, axis), (), 0, dims[axis]) for axis in range(len(dims))]
    array = array.at[tuple(place)].set(low)
    longest = dims.index(max(dims))
    place[longest] = (place[longest] + 1) % dims[longest]
    return array.at[tuple(place)].set(top_value)


def steps_of(rng, dims, shards, smallest, top_value):
    level = 1.0
    for dim, parts in shards:
        draws = jax.random.uniform(jax.random.fold_in(jax.random.fold_in(rng, 6), dim), (parts,), jnp.float32, smallest / len(shards), top_value / len(shards))
        level = level * jnp.repeat(jnp.exp(draws), dims[dim] // parts).reshape((-1,) + (1,) * (len(dims) - 1 - dim))
    return level


def noise(key, dims, scale, limit, shards=(), dtype=jnp.bfloat16):
    values = jax.random.normal(key, dims, jnp.float32) * scale
    if len(shards) > 0:
        values = steps_of(key, dims, shards, -0.22, 0.18) * values
    return jnp.clip(values, min=-limit, max=limit).astype(dtype)


def setup_inputs(seed: int = 0) -> dict:
    key_list = jax.random.split(jax.random.key(seed), 11)
    x_rows = noise(key_list[0], (TOKENS, D), 1.0, 6.0, ((0, 256),))
    out_grad = noise(key_list[1], (TOKENS, D), 1.0, 6.0, ((0, 256),))
    gate_codes = noise(key_list[2], (D, FF), 1.0, 4.0, ((1, 32),))
    gate_exps = touch_ends(jax.random.randint(key_list[3], (D // BLK_D, FF // BLK_F), -8, -4), jax.random.fold_in(key_list[3], 1), -8, (-4) - 1).astype(jnp.int32)
    up_codes = noise(key_list[4], (D, FF), 1.0, 4.0, ((1, 32),))
    up_exps = touch_ends(jax.random.randint(key_list[5], (D // BLK_D, FF // BLK_F), -8, -4), jax.random.fold_in(key_list[5], 1), -8, (-4) - 1).astype(jnp.int32)
    down_codes = noise(key_list[6], (FF, D), 1.0, 4.0, ((0, 32),))
    down_exps = touch_ends(jax.random.randint(key_list[7], (FF // BLK_F, D // BLK_D), -9, -5), jax.random.fold_in(key_list[7], 1), -9, (-5) - 1).astype(jnp.int32)
    replay_slot = touch_ends(jax.random.randint(key_list[8], (TOKENS,), 0, SLOTS), jax.random.fold_in(key_list[8], 1), 0, SLOTS - 1).astype(jnp.int32)
    priorities = jnp.clip(jnp.exp(jax.random.uniform(key_list[9], (SLOTS,), jnp.float32, math.log(0.01), math.log(1.0))), 0.01, 1.0)
    return dict(x_rows=x_rows, out_grad=out_grad, gate_codes=gate_codes, gate_exps=gate_exps, up_codes=up_codes, up_exps=up_exps, down_codes=down_codes, down_exps=down_exps, replay_slot=replay_slot, priorities=priorities)


def dequantize(codes, exponents):
    block_rows, block_cols = exponents.shape
    scales = jnp.exp2(exponents.astype(jnp.float32))
    values = codes.astype(jnp.float32).reshape(block_rows, codes.shape[0] // block_rows, block_cols, codes.shape[1] // block_cols)
    values = values * scales[:, None, :, None]
    return values.reshape(codes.shape).astype(jnp.bfloat16)

def contract(left, right, left_dim, right_dim):
    return lax.dot_general(left, right, (((left_dim,), (right_dim,)), ((), ())), preferred_element_type=jnp.float32)

def rounded(value):
    return lax.optimization_barrier(value.astype(jnp.bfloat16)).astype(jnp.float32)

def reference(x_rows, out_grad, gate_codes, gate_exps, up_codes, up_exps, down_codes, down_exps, replay_slot, priorities):
    w_gate = dequantize(gate_codes, gate_exps)
    w_up = dequantize(up_codes, up_exps)
    w_down = dequantize(down_codes, down_exps)
    total = jnp.sum(priorities)
    importance = lax.rsqrt(SLOTS * priorities[replay_slot] / total)
    groups = TOKENS // TOK_DEV
    x_groups = x_rows.reshape(groups, TOK_DEV, D)
    grad_groups = out_grad.reshape(groups, TOK_DEV, D)
    weight_groups = importance.reshape(groups, TOK_DEV)

    def group_step(carry, inputs):
        acc_gate, acc_up, acc_down = carry
        x_block, grad_block, weight_block = inputs
        gate = contract(x_block, w_gate, 1, 0)
        upper = contract(x_block, w_up, 1, 0)
        sigma = jax.nn.sigmoid(gate)
        active = gate * sigma
        hidden_grad = weight_block[:, None] * contract(grad_block, w_down, 1, 1)
        weighted_hidden = (weight_block[:, None] * active * upper).astype(jnp.bfloat16)
        up_delta = (hidden_grad * active).astype(jnp.bfloat16)
        gate_delta = (hidden_grad * upper * sigma * (1.0 + gate * (1.0 - sigma))).astype(jnp.bfloat16)
        input_block = (contract(gate_delta, w_gate, 1, 1) + contract(up_delta, w_up, 1, 1)).astype(jnp.bfloat16)
        acc_gate = acc_gate + rounded(contract(x_block, gate_delta, 0, 0))
        acc_up = acc_up + rounded(contract(x_block, up_delta, 0, 0))
        acc_down = acc_down + rounded(contract(weighted_hidden, grad_block, 0, 0))
        return ((acc_gate, acc_up, acc_down), input_block)
    start_carry = (jnp.zeros((D, FF), jnp.float32), jnp.zeros((D, FF), jnp.float32), jnp.zeros((FF, D), jnp.float32))
    final, input_blocks = lax.scan(group_step, start_carry, (x_groups, grad_groups, weight_groups))
    input_grad = input_blocks.reshape(TOKENS, D)
    return (input_grad, final[0].astype(jnp.bfloat16), final[1].astype(jnp.bfloat16), final[2].astype(jnp.bfloat16))
```

```python
import jax
import jax.numpy as jnp
from jax import lax
from jax.sharding import Mesh, PartitionSpec as P

ALL = ("x", "yl", "z", "yh", "core")
DP = ("x", "yl")
TENSOR = ("z", "yh", "core")


def dequantize(codes, exponents):
    block_rows, block_cols = exponents.shape
    scales = jnp.exp2(exponents.astype(jnp.float32))
    values = codes.astype(jnp.float32).reshape(
        block_rows, codes.shape[0] // block_rows, block_cols, codes.shape[1] // block_cols
    )
    values = values * scales[:, None, :, None]
    return values.reshape(codes.shape).astype(jnp.bfloat16)


def contract(left, right, left_dim, right_dim):
    return lax.dot_general(
        left, right, (((left_dim,), (right_dim,)), ((), ())), preferred_element_type=jnp.float32
    )


def shift(value, axis, step):
    size = lax.axis_size(axis)
    return lax.ppermute(value, axis, [(i, (i + step) % size) for i in range(size)])


def columns(value, index, width):
    return lax.dynamic_slice_in_dim(value, index * width, width, axis=1)


def gather_tensor(own):
    pair = jnp.concatenate([own, shift(own, "yh", 1)], axis=0)
    line = lax.all_gather(pair, "z", axis=0, tiled=True)
    return jnp.concatenate([line, shift(line, "core", 1)], axis=0)


def gather_x(own):
    left, right = shift(own, "x", 1), shift(own, "x", -1)
    half = own.shape[0] // 2
    far = jnp.concatenate([shift(left[:half], "x", 1), shift(right[half:], "x", -1)], axis=0)
    return own, left, right, far


def on_device(
    x_rows,
    out_grad,
    gate_codes,
    gate_exps,
    up_codes,
    up_exps,
    down_codes,
    down_exps,
    replay_slot,
    priorities,
):
    bf16 = jnp.bfloat16
    at_x, at_yl = lax.axis_index("x"), lax.axis_index("yl")
    at_yh, at_core = lax.axis_index("yh"), lax.axis_index("core")
    n_x = lax.axis_size("x")
    rows, width = x_rows.shape
    part = width // n_x
    both = jnp.concatenate([x_rows, out_grad], axis=0)
    sides = [
        shift(columns(both, (at_x + step) % n_x, part), "x", step) for step in (1, n_x - 1, 2)
    ]
    sides = jnp.concatenate(sides, axis=1)

    x_group = gather_tensor(x_rows)
    g_group = gather_tensor(out_grad)
    x_sides = gather_tensor(sides[:rows])
    g_sides = gather_tensor(sides[rows:])

    w_gate = dequantize(gate_codes, gate_exps)
    w_up = dequantize(up_codes, up_exps)
    w_down = dequantize(down_codes, down_exps)
    total = jnp.sum(priorities)
    importance = lax.rsqrt(priorities.shape[0] * jnp.take(priorities, replay_slot) / total)
    importance = importance.reshape(-1, 2, 2, rows)
    importance = jnp.where(at_yh == 1, importance[:, ::-1], importance)
    importance = jnp.where(at_core == 1, importance[:, :, ::-1], importance)
    importance = importance.transpose(2, 0, 1, 3).reshape(-1, 1)

    gate = contract(x_group, w_gate, 1, 0)
    upper = contract(x_group, w_up, 1, 0)
    sigma = jax.nn.sigmoid(gate)
    active = gate * sigma
    weighted_hidden = (importance * active * upper).astype(bf16)
    hidden_grad = importance * contract(g_group, w_down, 1, 1)
    up_delta = (hidden_grad * active).astype(bf16)
    gate_delta = (hidden_grad * upper * sigma * (1.0 + gate * (1.0 - sigma))).astype(bf16)

    hidden_all = gather_x(weighted_hidden)
    gate_all = gather_x(gate_delta)
    up_all = gather_x(up_delta)

    partial = contract(gate_delta, w_gate, 1, 1) + contract(up_delta, w_up, 1, 1)
    half = partial.shape[0] // 2
    mine = partial[:half] + shift(partial[half:].astype(bf16), "core", 1)
    line = lax.psum_scatter(mine.astype(bf16), "z", scatter_dimension=0, tiled=True)
    other = shift(line[rows:], "yh", 1)
    input_grad = (line[:rows].astype(jnp.float32) + other.astype(jnp.float32)).astype(bf16)

    def weight_grad(blocks, group, others, lhs_is_block):
        pieces = [columns(group, at_x, part)] + [
            others[:, i * part : (i + 1) * part] for i in range(n_x - 1)
        ]
        pieces = jnp.concatenate(pieces, axis=0)
        blocks = jnp.concatenate(blocks, axis=0)
        dim = 1 if lhs_is_block else 0
        if lhs_is_block:
            value = contract(blocks, pieces, 0, 0)
        else:
            value = contract(pieces, blocks, 0, 0)
        size = part // 2
        keep = lax.dynamic_slice_in_dim(value, at_yl * size, size, axis=dim)
        send = lax.dynamic_slice_in_dim(value, (1 - at_yl) * size, size, axis=dim)
        return (keep + shift(send.astype(bf16), "yl", 1).astype(jnp.float32)).astype(bf16)

    grad_down = weight_grad(hidden_all, g_group, g_sides, True)
    grad_gate = weight_grad(gate_all, x_group, x_sides, False)
    grad_up = weight_grad(up_all, x_group, x_sides, False)
    return input_grad, grad_gate, grad_up, grad_down


def solution(mesh):
    fine = Mesh(mesh.devices.reshape(4, 2, 8, 2, 2), ALL)
    return jax.shard_map(
        on_device,
        mesh=fine,
        in_specs=(
            P(ALL, None),
            P(ALL, None),
            P(None, TENSOR),
            P(None, TENSOR),
            P(None, TENSOR),
            P(None, TENSOR),
            P(TENSOR, None),
            P(TENSOR, None),
            P(DP),
            P(),
        ),
        out_specs=(
            P(ALL, None),
            P(DP, TENSOR),
            P(DP, TENSOR),
            P(TENSOR, DP),
        ),
        check_vma=False,
    )
```

```python
import functools

import jax
import jax.numpy as jnp
from jax import lax
from jax.experimental import pallas as pl
from jax.experimental.pallas import tpu as pltpu
from jax.sharding import Mesh, PartitionSpec as P

ALL = ("x", "yl", "z", "yh", "core")
DP = ("x", "yl")
TENSOR = ("z", "yh", "core")
STEP = 512
SPLIT = 240
f32, bf16 = jnp.float32, jnp.bfloat16


def params(mib=48):
    return pltpu.CompilerParams(vmem_limit_bytes=mib * 2**20)


def cost(flops, nbytes):
    return pl.CostEstimate(flops=flops, bytes_accessed=nbytes, transcendentals=0)


def dequantize(codes, exponents):
    block_rows, block_cols = exponents.shape
    scales = jnp.exp2(exponents.astype(f32))
    values = codes.astype(f32).reshape(
        block_rows, codes.shape[0] // block_rows, block_cols, codes.shape[1] // block_cols
    )
    values = values * scales[:, None, :, None]
    return values.reshape(codes.shape).astype(bf16)


def pad_to(value, dim, size):
    widths = [(0, 0), (0, 0)]
    widths[dim] = (0, size - value.shape[dim])
    return jnp.pad(value, widths)


def dot(left, right, left_dim, right_dim):
    return lax.dot_general(
        left, right, (((left_dim,), (right_dim,)), ((), ())), preferred_element_type=f32
    )


def stack(first, second):
    return jnp.concatenate([first[...], second[...]], axis=0)


def shift(value, axis, step):
    size = lax.axis_size(axis)
    return lax.ppermute(value, axis, [(i, (i + step) % size) for i in range(size)])


def columns(value, index, width):
    return lax.dynamic_slice_in_dim(value, index * width, width, axis=1)


def forward_body(xa, xb, wg, wu, imp, hidden_t, active, slope, gate_acc, up_acc):
    step = pl.program_id(0)
    rows = stack(xa, xb)
    gate_part = dot(rows, wg[...], 1, 0)
    up_part = dot(rows, wu[...], 1, 0)

    @pl.when(step == 0)
    def _():
        gate_acc[...] = gate_part
        up_acc[...] = up_part

    @pl.when(step > 0)
    def _():
        gate_acc[...] += gate_part
        up_acc[...] += up_part

    @pl.when(step == pl.num_programs(0) - 1)
    def _():
        gate, up = gate_acc[...], up_acc[...]
        sigma = jax.nn.sigmoid(gate)
        act = gate * sigma
        active[...] = act
        slope[...] = up * sigma * (1.0 + gate * (1.0 - sigma))
        hidden = imp[...] * act * up
        hidden_t[...] = hidden.T[: hidden_t.shape[0]].astype(bf16)


def forward(xa, xb, wg, wu, imp, hidden):
    half, width = xa.shape
    tokens, pad = 2 * half, wg.shape[1]
    return pl.pallas_call(
        forward_body,
        grid=(width // STEP,),
        in_specs=[
            pl.BlockSpec((half, STEP), lambda k: (0, k)),
            pl.BlockSpec((half, STEP), lambda k: (0, k)),
            pl.BlockSpec((STEP, pad), lambda k: (k, 0)),
            pl.BlockSpec((STEP, pad), lambda k: (k, 0)),
            pl.BlockSpec((tokens, 1), lambda k: (0, 0)),
        ],
        out_specs=[
            pl.BlockSpec((hidden, tokens), lambda k: (0, 0)),
            pl.BlockSpec((tokens, pad), lambda k: (0, 0)),
            pl.BlockSpec((tokens, pad), lambda k: (0, 0)),
        ],
        out_shape=[
            jax.ShapeDtypeStruct((hidden, tokens), bf16),
            jax.ShapeDtypeStruct((tokens, pad), f32),
            jax.ShapeDtypeStruct((tokens, pad), f32),
        ],
        scratch_shapes=[pltpu.VMEM((tokens, pad), f32)] * 2,
        compiler_params=params(),
        cost_estimate=cost(4 * tokens * width * pad, 14 * 2**20),
        name="forward",
    )(xa, xb, wg, wu, imp)


def delta_body(ga, gb, wd, imp, active, slope, gate_t, up_t, gate_d, up_d, acc):
    step = pl.program_id(0)
    part = dot(stack(ga, gb), wd[...], 1, 1)

    @pl.when(step == 0)
    def _():
        acc[...] = part

    @pl.when(step > 0)
    def _():
        acc[...] += part

    @pl.when(step == pl.num_programs(0) - 1)
    def _():
        grad = imp[...] * acc[...]
        up = grad * active[...]
        gate = grad * slope[...]
        up_d[...] = up.astype(bf16)
        gate_d[...] = gate.astype(bf16)
        gate_t[...] = gate.T[: gate_t.shape[0]].astype(bf16)
        up_t[...] = up.T[: up_t.shape[0]].astype(bf16)


def deltas(ga, gb, wd, imp, active, slope, hidden):
    half, width = ga.shape
    tokens, pad = 2 * half, wd.shape[0]
    whole = pl.BlockSpec((tokens, pad), lambda k: (0, 0))
    flat = pl.BlockSpec((hidden, tokens), lambda k: (0, 0))
    return pl.pallas_call(
        delta_body,
        grid=(width // STEP,),
        in_specs=[
            pl.BlockSpec((half, STEP), lambda k: (0, k)),
            pl.BlockSpec((half, STEP), lambda k: (0, k)),
            pl.BlockSpec((pad, STEP), lambda k: (0, k)),
            pl.BlockSpec((tokens, 1), lambda k: (0, 0)),
            whole,
            whole,
        ],
        out_specs=[flat, flat, whole, whole],
        out_shape=[
            jax.ShapeDtypeStruct((hidden, tokens), bf16),
            jax.ShapeDtypeStruct((hidden, tokens), bf16),
            jax.ShapeDtypeStruct((tokens, pad), bf16),
            jax.ShapeDtypeStruct((tokens, pad), bf16),
        ],
        scratch_shapes=[pltpu.VMEM((tokens, pad), f32)],
        compiler_params=params(),
        cost_estimate=cost(2 * tokens * width * pad, 11 * 2**20),
        name="deltas",
    )(ga, gb, wd, imp, active, slope)


def input_body(gate_d, up_d, wg, wu, own, send):
    half = own.shape[0]
    value = dot(gate_d[...], wg[...], 1, 1) + dot(up_d[...], wu[...], 1, 1)
    own[...] = value[:half]
    send[...] = value[half:].astype(bf16)


def input_partial(gate_d, up_d, wg, wu):
    tokens, pad = gate_d.shape
    width, half = wg.shape[0], tokens // 2
    whole = pl.BlockSpec((tokens, pad), lambda k: (0, 0))
    weight = pl.BlockSpec((STEP, pad), lambda k: (k, 0))
    out = pl.BlockSpec((half, STEP), lambda k: (0, k))
    return pl.pallas_call(
        input_body,
        grid=(width // STEP,),
        in_specs=[whole, whole, weight, weight],
        out_specs=[out, out],
        out_shape=[
            jax.ShapeDtypeStruct((half, width), f32),
            jax.ShapeDtypeStruct((half, width), bf16),
        ],
        compiler_params=params(),
        cost_estimate=cost(4 * tokens * width * pad, 14 * 2**20),
        name="input_partial",
    )(gate_d, up_d, wg, wu)


def weight_body(where, xa, xb, *refs):
    sides, (own, left, right, far_a, far_b, out) = refs[:6], refs[6:]
    value = dot(own[...], stack(xa, xb), 1, 0)
    value += dot(left[...], stack(sides[0], sides[1]), 1, 0)
    value += dot(right[...], stack(sides[2], sides[3]), 1, 0)
    value += dot(stack(far_a, far_b), stack(sides[4], sides[5]), 1, 0)
    out[...] = value.astype(out.dtype)


def weight_part(where, xa, xb, sa, sb, blocks, first, dtype):
    half, width = xa.shape
    hidden, tokens = blocks[0].shape
    size = 256
    part = width // 8
    per = part // size
    group = pl.BlockSpec((half, size), lambda j, w: (0, (2 * w[0] + w[1]) * per + j))

    def side(i):
        return pl.BlockSpec((half, size), lambda j, w: (0, (first + 2 * i + w[1]) * per + j))

    def whole(rows):
        return pl.BlockSpec((rows, tokens), lambda j, w: (0, 0))

    return pl.pallas_call(
        weight_body,
        grid_spec=pltpu.PrefetchScalarGridSpec(
            num_scalar_prefetch=1,
            grid=(per,),
            in_specs=[group, group]
            + [side(i) for i in (0, 0, 1, 1, 2, 2)]
            + [whole(b.shape[0]) for b in blocks],
            out_specs=pl.BlockSpec((hidden, size), lambda j, w: (0, j)),
        ),
        out_shape=jax.ShapeDtypeStruct((hidden, part), dtype),
        compiler_params=params(),
        cost_estimate=cost(2 * 4 * tokens * hidden * part, 4 * 2**20),
        name="weight_part",
    )(where, xa, xb, sa, sb, sa, sb, sa, sb, *blocks)


def final_body(keep, received, out, *, turn):
    value = keep[...] + received[...].astype(f32)
    out[...] = (value.T if turn else value).astype(bf16)


def final_sum(keep, received, turn):
    hidden, part = keep.shape
    size = 128
    block = pl.BlockSpec((hidden, size), lambda j: (0, j))
    return pl.pallas_call(
        functools.partial(final_body, turn=turn),
        grid=(part // size,),
        in_specs=[block, block],
        out_specs=pl.BlockSpec((size, hidden), lambda j: (j, 0)) if turn else block,
        out_shape=jax.ShapeDtypeStruct((part, hidden) if turn else (hidden, part), bf16),
        compiler_params=params(),
        cost_estimate=cost(hidden * part, 2 * 2**20),
        name="final_sum",
    )(keep, received)


def ring_gather(own, at_z):
    n = lax.axis_size("z")
    buffer = jnp.zeros((n,) + own.shape, own.dtype)

    def put(buffer, block, offset):
        return lax.dynamic_update_slice(buffer, block[None], ((at_z + offset) % n, 0, 0))

    buffer = put(buffer, own, 0)
    left = right = own
    for step in range(1, n // 2):
        left, right = shift(left, "z", 1), shift(right, "z", -1)
        buffer = put(put(buffer, left, n - step), right, step)
    cols = own.shape[1] // 2
    left = shift(left[:, :cols], "z", 1)
    right = shift(right[:, cols:], "z", -1)
    buffer = put(buffer, jnp.concatenate([left, right], axis=1), n // 2)
    return buffer.reshape(-1, own.shape[1])


def ring_scatter(parts, at_z):
    n = lax.axis_size("z")
    cols = parts.shape[2] // 2

    def block(offset):
        return lax.dynamic_index_in_dim(parts, (at_z + offset) % n, 0, keepdims=False)

    far = block(n // 2)
    left, right = shift(far[:, cols:], "z", -1), shift(far[:, :cols], "z", 1)
    for step in range(n // 2 - 1, 0, -1):
        to_right, to_left = block(step).astype(f32), block(n - step).astype(f32)
        if step == n // 2 - 1:
            right = jnp.pad(right, ((0, 0), (0, cols)))
            left = jnp.pad(left, ((0, 0), (cols, 0)))
        right = shift((to_right + right.astype(f32)).astype(bf16), "z", 1)
        left = shift((to_left + left.astype(f32)).astype(bf16), "z", -1)
    return block(0).astype(f32) + left.astype(f32) + right.astype(f32)


def gather_x(own):
    left, right = shift(own, "x", 1), shift(own, "x", -1)
    return own, left, right, shift(left[:SPLIT], "x", 1), shift(right[SPLIT:], "x", -1)


def on_device(
    x_rows,
    out_grad,
    gate_codes,
    gate_exps,
    up_codes,
    up_exps,
    down_codes,
    down_exps,
    replay_slot,
    priorities,
):
    at_x, at_yl = lax.axis_index("x"), lax.axis_index("yl")
    at_z, at_yh, at_core = lax.axis_index("z"), lax.axis_index("yh"), lax.axis_index("core")
    n_x = lax.axis_size("x")
    rows, width = x_rows.shape
    hidden = gate_codes.shape[1]
    pad = -(-hidden // 128) * 128
    part = width // n_x

    x_pair = jnp.concatenate([x_rows, shift(x_rows, "yh", 1)], axis=0)
    g_pair = jnp.concatenate([out_grad, shift(out_grad, "yh", 1)], axis=0)
    both = jnp.concatenate([x_rows, out_grad], axis=0)
    sides = [
        shift(columns(both, (at_x + step) % n_x, part), "x", step) for step in (1, n_x - 1, 2)
    ]
    sides = jnp.concatenate([s[:rows] for s in sides] + [s[rows:] for s in sides], axis=1)
    sides = jnp.concatenate([sides, shift(sides, "yh", 1)], axis=0)

    w_gate = pad_to(dequantize(gate_codes, gate_exps), 1, pad)
    w_up = pad_to(dequantize(up_codes, up_exps), 1, pad)
    w_down = pad_to(dequantize(down_codes, down_exps), 0, pad)
    total = jnp.sum(priorities)
    importance = lax.rsqrt(priorities.shape[0] * jnp.take(priorities, replay_slot) / total)
    importance = importance.reshape(-1, 2, 2, rows)
    importance = jnp.where(at_yh == 1, importance[:, ::-1], importance)
    importance = jnp.where(at_core == 1, importance[:, :, ::-1], importance)
    importance = importance.transpose(2, 0, 1, 3).reshape(-1, 1)

    xa = ring_gather(x_pair, at_z)
    ga = ring_gather(g_pair, at_z)
    xb = shift(xa, "core", 1)
    sides, xa = lax.optimization_barrier((sides, xa))
    sa = lax.all_gather(sides, "z", axis=0, tiled=True)
    gb = shift(ga, "core", 1)

    hidden_t, active, slope = forward(xa, xb, w_gate, w_up, importance, hidden)
    hidden_all = gather_x(hidden_t)
    gate_t, up_t, gate_d, up_d = deltas(ga, gb, w_down, importance, active, slope, hidden)
    gate_all = gather_x(gate_t)
    up_all = gather_x(up_t)

    own, send = input_partial(gate_d, up_d, w_gate, w_up)
    mine = (own + shift(send, "core", 1).astype(f32)).astype(bf16)
    line = ring_scatter(mine.reshape(-1, 2 * rows, width), at_z)
    other = shift(line[rows:].astype(bf16), "yh", 1)
    input_grad = (line[:rows] + other.astype(f32)).astype(bf16)

    sb = shift(sa, "core", 1)
    send_at = jnp.stack([at_x, 1 - at_yl]).astype(jnp.int32)
    keep_at = jnp.stack([at_x, at_yl]).astype(jnp.int32)

    def weight_grad(blocks, a, b, first, turn):
        send = weight_part(send_at, a, b, sa, sb, blocks, first, bf16)
        received = shift(send, "yl", 1)
        keep = weight_part(keep_at, a, b, sa, sb, blocks, first, f32)
        return final_sum(keep, received, turn)

    grad_down = weight_grad(hidden_all, ga, gb, 2 * (n_x - 1), False)
    grad_gate = weight_grad(gate_all, xa, xb, 0, True)
    grad_up = weight_grad(up_all, xa, xb, 0, True)
    return input_grad, grad_gate, grad_up, grad_down


def solution(mesh):
    fine = Mesh(mesh.devices.reshape(4, 2, 8, 2, 2), ALL)
    return jax.shard_map(
        on_device,
        mesh=fine,
        in_specs=(
            P(ALL, None),
            P(ALL, None),
            P(None, TENSOR),
            P(None, TENSOR),
            P(None, TENSOR),
            P(None, TENSOR),
            P(TENSOR, None),
            P(TENSOR, None),
            P(DP),
            P(),
        ),
        out_specs=(
            P(ALL, None),
            P(DP, TENSOR),
            P(DP, TENSOR),
            P(TENSOR, DP),
        ),
        check_vma=False,
    )
```

```python
import functools

import jax
import jax.numpy as jnp
from jax import lax
from jax.experimental import pallas as pl
from jax.experimental.pallas import tpu as pltpu
from jax.sharding import Mesh, PartitionSpec as P

ALL = ("x", "yl", "z", "yh", "core")
DP = ("x", "yl")
TENSOR = ("z", "yh", "core")
WIDE = 1024
LANES = 128
SPLIT = 240
f32, bf16 = jnp.float32, jnp.bfloat16


def params(mib):
    return pltpu.CompilerParams(vmem_limit_bytes=mib * 2**20)


def cost(us):
    return pl.CostEstimate(flops=2**20, bytes_accessed=int(us * 3e6), transcendentals=0)


def dot(left, right, left_dim, right_dim):
    return lax.dot_general(
        left, right, (((left_dim,), (right_dim,)), ((), ())), preferred_element_type=f32
    )


def stack(first, second):
    return jnp.concatenate([first[...], second[...]], axis=0)


def shift(value, axis, step):
    size = lax.axis_size(axis)
    return lax.ppermute(value, axis, [(i, (i + step) % size) for i in range(size)])


def columns(value, index, width):
    return lax.dynamic_slice_in_dim(value, index * width, width, axis=1)


def dequantize_body(codes, exps, out, *, turned):
    rows, size = codes.shape
    step = pl.program_id(0)
    scale = jnp.exp2(exps[...].astype(f32)).astype(bf16)
    blocks = scale.shape[0 if turned else 1]
    at = lax.broadcasted_iota(jnp.int32, (blocks, size), 1) // LANES + step * (size // LANES)
    spread = (at == lax.broadcasted_iota(jnp.int32, (blocks, size), 0)).astype(f32).astype(bf16)
    wide = dot(scale, spread, 0 if turned else 1, 0)
    groups = wide.shape[0]
    wide = jnp.broadcast_to(wide[:, None, :], (groups, rows // groups, size))
    wide = wide.reshape(rows, size)
    out[:rows] = (codes[...].astype(f32) * wide).astype(bf16)
    out[rows:] = jnp.zeros((out.shape[0] - rows, size), bf16)


def dequantize(codes, exps, pad, turned):
    hidden, width = codes.shape
    return pl.pallas_call(
        functools.partial(dequantize_body, turned=turned),
        grid=(width // WIDE,),
        in_specs=[
            pl.BlockSpec((hidden, WIDE), lambda k: (0, k)),
            pl.BlockSpec(exps.shape, lambda k: (0, 0)),
        ],
        out_specs=pl.BlockSpec((pad, WIDE), lambda k: (0, k)),
        out_shape=jax.ShapeDtypeStruct((pad, width), bf16),
        compiler_params=params(24),
        cost_estimate=cost(5),
        name="dequantize",
    )(codes, exps)


def forward_body(main, wg, wu, wd, imp, *refs, hidden):
    first = refs[:3] if hidden else ()
    outs, (main_s, weights_s, sems) = refs[len(first) : -3], refs[-3:]
    width = wg.shape[1]
    chunks = width // WIDE

    def copies(c):
        at, g_at = pl.ds(c * WIDE, WIDE), pl.ds(width + c * WIDE, WIDE)
        pairs = [
            (main.at[:, at], main_s.at[:, at]),
            (wg.at[:, at], weights_s.at[0, :, at]),
            (wu.at[:, at], weights_s.at[1, :, at]),
            (main.at[:, g_at], main_s.at[:, g_at]),
            (wd.at[:, at], weights_s.at[2, :, at]),
        ]
        return [
            pltpu.make_async_copy(source, target, sems.at[c, i])
            for i, (source, target) in enumerate(pairs)
        ]

    for c in range(chunks):
        for copy in copies(c):
            copy.start()
    gate = up = grad = 0.0
    for c in range(chunks):
        at, g_at = pl.ds(c * WIDE, WIDE), pl.ds(width + c * WIDE, WIDE)
        for copy in copies(c):
            copy.wait()
        x = main_s[:, at]
        gate += dot(x, weights_s[0, :, at], 1, 1)
        up += dot(x, weights_s[1, :, at], 1, 1)
        grad += dot(main_s[:, g_at], weights_s[2, :, at], 1, 1)
    grad = imp[...] * grad
    sigma = jax.nn.sigmoid(gate)
    act = gate * sigma
    hid = (imp[...] * act * up).astype(bf16)
    up_delta = (grad * act).astype(bf16)
    gate_delta = (grad * up * sigma * (1.0 + gate * (1.0 - sigma))).astype(bf16)
    values = hid, gate_delta, up_delta
    if hidden:
        for out, before, value in zip(outs, first, values):
            rows = jnp.concatenate([before[...], value], axis=0)
            out[...] = rows.astype(f32).T[:hidden].astype(bf16)
    else:
        for out, value in zip(outs, values):
            out[...] = value
    partial = outs[3]
    for c in range(chunks):
        at = pl.ds(c * WIDE, WIDE)
        value = dot(gate_delta, weights_s[0, :, at], 1, 0)
        value += dot(up_delta, weights_s[1, :, at], 1, 0)
        partial[:, at] = value.astype(partial.dtype)


def forward(main, weights, imp, half_at, first=(), hidden=0):
    half, columns_in = main.shape
    pad, width = weights[0].shape
    whole = pl.BlockSpec(memory_space=pl.ANY)
    rows = pl.BlockSpec((half, pad), lambda k: (0, 0))
    sent = pl.BlockSpec((hidden, 2 * half), lambda k: (0, 0)) if hidden else rows
    shape = (hidden, 2 * half) if hidden else (half, pad)
    return pl.pallas_call(
        functools.partial(forward_body, hidden=hidden),
        grid=(1,),
        in_specs=[whole] * 4
        + [pl.BlockSpec((half, 1), lambda k: (half_at, 0))]
        + [rows] * len(first),
        out_specs=[sent] * 3 + [pl.BlockSpec((half, width), lambda k: (0, 0))],
        out_shape=[jax.ShapeDtypeStruct(shape, bf16)] * 3
        + [jax.ShapeDtypeStruct((half, width), bf16 if hidden else f32)],
        scratch_shapes=[
            pltpu.VMEM((half, columns_in), bf16),
            pltpu.VMEM((3, pad, width), bf16),
            pltpu.SemaphoreType.DMA((width // WIDE, 5)),
        ],
        compiler_params=params(48),
        cost_estimate=cost(9),
        name="forward",
    )(main, *weights, imp, *first)


def input_body(where, own, received, out):
    out[...] = (own[...] + received[...].astype(f32)).astype(bf16)


def input_sum(where, own, received):
    n, rows, width = own.shape
    block = pl.BlockSpec((1, rows, width), lambda i, w: (i, 0, 0))
    return pl.pallas_call(
        input_body,
        grid_spec=pltpu.PrefetchScalarGridSpec(
            num_scalar_prefetch=1,
            grid=(n,),
            in_specs=[block, block],
            out_specs=pl.BlockSpec((1, rows, width), lambda i, w: (w[i], 0, 0)),
        ),
        out_shape=jax.ShapeDtypeStruct(own.shape, bf16),
        compiler_params=params(16),
        cost_estimate=cost(3),
        name="input_sum",
    )(where, own, received)


def weight_body(where, xa, xb, *refs):
    sides, blocks, (far_a, far_b, send, keep) = refs[:6], refs[6:9], refs[9:]
    rows = jnp.concatenate([r[...] for r in (xa, xb, *sides)], axis=0)
    blocks = [b[...] for b in blocks] + [stack(far_a, far_b)]
    value = dot(jnp.concatenate(blocks, axis=1), rows, 1, 0)
    step, per = pl.program_id(0), pl.num_programs(0) // 2

    @pl.when(step < per)
    def _():
        send[...] = value.astype(bf16)

    @pl.when(step >= per)
    def _():
        keep[...] = value


def weight_part(where, main_a, main_b, sides, blocks, second, part):
    half = main_a.shape[0]
    hidden, tokens = blocks[0].shape
    size = 512
    per = part // size

    def spot(first, j, w):
        return (first + w[1 + j // per]) * per + j % per

    group = pl.BlockSpec((half, size), lambda j, w: (0, spot(8 * second + 2 * w[0], j, w)))
    side = pl.BlockSpec((half, size), lambda j, w: (0, spot(2 * second, j, w)))
    return pl.pallas_call(
        weight_body,
        grid_spec=pltpu.PrefetchScalarGridSpec(
            num_scalar_prefetch=1,
            grid=(2 * per,),
            in_specs=[group, group]
            + [side] * 6
            + [pl.BlockSpec(b.shape, lambda j, w: (0, 0)) for b in blocks],
            out_specs=[
                pl.BlockSpec((hidden, size), lambda j, w: (0, jnp.minimum(j, per - 1))),
                pl.BlockSpec((hidden, size), lambda j, w: (0, jnp.maximum(j - per, 0))),
            ],
        ),
        out_shape=[
            jax.ShapeDtypeStruct((hidden, part), bf16),
            jax.ShapeDtypeStruct((hidden, part), f32),
        ],
        compiler_params=params(56),
        cost_estimate=cost(6),
        name="weight_part",
    )(where, main_a, main_b, *sides, *blocks)


def after(value, earlier):
    return lax.optimization_barrier((value, earlier))[0]


def on_device(
    x_rows,
    out_grad,
    gate_codes,
    gate_exps,
    up_codes,
    up_exps,
    down_codes,
    down_exps,
    replay_slot,
    priorities,
):
    at_x, at_yl = lax.axis_index("x"), lax.axis_index("yl")
    at_z, at_yh, at_core = lax.axis_index("z"), lax.axis_index("yh"), lax.axis_index("core")
    n_x = lax.axis_size("x")
    rows, width = x_rows.shape
    hidden = down_codes.shape[0]
    pad = -(-hidden // LANES) * LANES
    line_part = width // n_x
    part = line_part // lax.axis_size("yl")

    def weigh_tokens(slots):
        total = jnp.sum(priorities)
        importance = lax.rsqrt(priorities.shape[0] * jnp.take(priorities, slots) / total)
        importance = importance.reshape(-1, 2, 2, rows)
        importance = jnp.where(at_yh == 1, importance[:, ::-1], importance)
        importance = jnp.where(at_core == 1, importance[:, :, ::-1], importance)
        importance = jnp.roll(importance, -at_z, axis=0)
        importance = jnp.stack([importance[i] for i in (0, 7, 1, 6, 2, 5, 3, 4)])
        return importance.transpose(2, 0, 1, 3).reshape(-1, 1)

    def both_ways(left, right):
        return shift(left, "z", 1), shift(right, "z", -1)

    together = lax.optimization_barrier

    def cut(blocks):
        group = jnp.stack(blocks).reshape(-1, 2 * width)
        spots = [(at_x + step) % n_x for step in steps]
        return [
            jnp.concatenate(
                [columns(group, spot, line_part), columns(group, spot + n_x, line_part)], axis=1
            )
            for spot in spots
        ]

    def swap_sides(slices):
        return [shift(piece, "x", step) for piece, step in zip(slices, steps)]

    steps = (1, n_x - 1, 2)

    others = shift(x_rows, "yh", 1), shift(out_grad, "yh", 1)
    main = jnp.concatenate(
        [jnp.concatenate([x_rows, out_grad], axis=1), jnp.concatenate(others, axis=1)], axis=0
    )

    ring1 = both_ways(main, main)
    w_gate = dequantize(after(gate_codes.T, main), gate_exps, pad, True)
    ring1, w_gate = together((ring1, w_gate))

    ring2 = both_ways(*ring1)
    w_up = dequantize(after(up_codes.T, ring1), up_exps, pad, True)
    ring2, w_up = together((ring2, w_up))

    ring3 = both_ways(*ring2)
    near_sides = swap_sides(cut([main, *ring1, *ring2]))
    w_down = dequantize(after(down_codes, ring2), down_exps, pad, False)
    ring3, w_down = together((ring3, w_down))

    far = both_ways(ring3[0][:, :width], ring3[1][:, width:])
    importance = weigh_tokens(after(replay_slot, ring3))
    far, importance, near_sides = together((far, importance, near_sides))

    far = jnp.concatenate(far, axis=1)
    main_a = jnp.stack([main, *ring1, *ring2, *ring3, far]).reshape(-1, 2 * width)
    main_b = shift(main_a, "core", 1)
    slices = cut([*ring3, far])
    far_sides = swap_sides(slices)
    weights = w_gate, w_up, w_down
    first = forward(main_a, weights, importance, 0)
    main_b, far_sides, first = together((main_b, far_sides, first))
    *first, own = first
    hid_t, gate_t, up_t, send = forward(main_b, weights, importance, 1, first, hidden)

    def along_x(block):
        return shift(block, "x", 1), shift(block, "x", -1)

    def along_x_far(left, right):
        return shift(left[:SPLIT], "x", 1), shift(right[SPLIT:], "x", -1)

    hid_near = along_x(hid_t)
    received = shift(send, "core", 1)
    sides = [jnp.concatenate(s, axis=0) for s in zip(near_sides, far_sides)]
    hid_near, received, sides = together((hid_near, received, sides))

    hid_far = along_x_far(*hid_near)
    gate_near = along_x(gate_t)
    spots = (at_z + jnp.array([0, 7, 1, 6, 2, 5, 3, 4], jnp.int32)) % 8
    own, received = [v.reshape(len(spots), -1, width) for v in (own, received)]
    line = input_sum(spots.astype(jnp.int32), own, received)
    sides = [s for side in sides for s in (side, shift(side, "core", 1))]
    hid_far, gate_near, sides, line = together((hid_far, gate_near, sides, line))
    line = lax.all_to_all(line, "z", 0, 0, tiled=True)

    where = jnp.stack([at_x, 1 - at_yl, at_yl]).astype(jnp.int32)

    def weight_grad(blocks, second):
        return weight_part(where, main_a, main_b, sides, blocks, second, part)

    gate_far = along_x_far(*gate_near)
    up_near = along_x(up_t)
    down = weight_grad((hid_t, *hid_near, *hid_far), 1)
    gate_far, up_near, down = together((gate_far, up_near, down))

    up_far = along_x_far(*up_near)
    down_got = shift(down[0], "yl", 1)
    gate = weight_grad((gate_t, *gate_near, *gate_far), 0)
    up_far, gate = together((up_far, gate))
    gate, down_got = together((gate, down_got))

    gate_got = shift(gate[0], "yl", 1)
    up = weight_grad((up_t, *up_near, *up_far), 0)
    up, gate_got = together((up, gate_got))
    up_got = shift(up[0], "yl", 1)
    line = jnp.sum(after(line, up).astype(f32), axis=0)
    other = shift(line[rows:].astype(bf16), "yh", 1)
    grad_down = (down[1] + down_got.astype(f32)).astype(bf16)
    grad_gate = (gate[1] + gate_got.astype(f32)).astype(bf16).T
    input_grad = (line[:rows] + other.astype(f32)).astype(bf16)
    grad_up = (up[1] + up_got.astype(f32)).astype(bf16).T
    return input_grad, grad_gate, grad_up, grad_down


def solution(mesh):
    fine = Mesh(mesh.devices.reshape(4, 2, 8, 2, 2), ALL)
    return jax.shard_map(
        on_device,
        mesh=fine,
        in_specs=(
            P(ALL, None),
            P(ALL, None),
            P(None, TENSOR),
            P(None, TENSOR),
            P(None, TENSOR),
            P(None, TENSOR),
            P(TENSOR, None),
            P(TENSOR, None),
            P(DP),
            P(),
        ),
        out_specs=(
            P(ALL, None),
            P(DP, TENSOR),
            P(DP, TENSOR),
            P(TENSOR, DP),
        ),
        check_vma=False,
    )
```

```python
import functools

import jax
import jax.numpy as jnp
from jax import lax
from jax.experimental import pallas as pl
from jax.experimental.pallas import tpu as pltpu
from jax.sharding import Mesh, PartitionSpec as P

ALL = ("x", "yl", "z", "yh", "core")
DP = ("x", "yl")
TENSOR = ("z", "yh", "core")
WIDE = 1024
LANES = 128
SPLIT = 240
f32, bf16 = jnp.float32, jnp.bfloat16


def params(mib):
    return pltpu.CompilerParams(vmem_limit_bytes=mib * 2**20)


def cost(us):
    return pl.CostEstimate(flops=2**20, bytes_accessed=int(us * 3e6), transcendentals=0)


def dot(left, right, left_dim, right_dim):
    return lax.dot_general(
        left, right, (((left_dim,), (right_dim,)), ((), ())), preferred_element_type=f32
    )


def stack(first, second):
    return jnp.concatenate([first[...], second[...]], axis=0)


def shift(value, axis, step):
    size = lax.axis_size(axis)
    return lax.ppermute(value, axis, [(i, (i + step) % size) for i in range(size)])


def columns(value, index, width):
    return lax.dynamic_slice_in_dim(value, index * width, width, axis=1)


def dequantized(codes, exps, chunk, turned):
    rows, size = codes.shape
    scale = jnp.exp2(exps[...].astype(f32)).astype(bf16)
    blocks = scale.shape[0 if turned else 1]
    at = lax.broadcasted_iota(jnp.int32, (blocks, size), 1) // LANES + chunk * (size // LANES)
    spread = (at == lax.broadcasted_iota(jnp.int32, (blocks, size), 0)).astype(f32).astype(bf16)
    wide = dot(scale, spread, 0 if turned else 1, 0)
    groups = wide.shape[0]
    wide = jnp.broadcast_to(wide[:, None, :], (groups, rows // groups, size))
    return (codes.astype(f32) * wide.reshape(rows, size)).astype(bf16)


def forward_body(
    main_a, main_b, gate_codes, up_codes, down_codes, ge, ue, de, imp, *refs
):
    outs, (own, send, main_s, codes_s, weights_s, sems) = refs[:3], refs[3:]
    rows, width = gate_codes.shape
    half = main_a.shape[0]
    chunks = width // WIDE

    def copies(c):
        at, g_at = pl.ds(c * WIDE, WIDE), pl.ds(width + c * WIDE, WIDE)
        first, second = pl.ds(0, half), pl.ds(half, half)
        pairs = [
            (gate_codes.at[:, at], codes_s.at[0, :, at]),
            (main_a.at[:, at], main_s.at[first, at]),
            (main_b.at[:, at], main_s.at[second, at]),
            (up_codes.at[:, at], codes_s.at[1, :, at]),
            (down_codes.at[:, at], codes_s.at[2, :, at]),
            (main_a.at[:, g_at], main_s.at[first, g_at]),
            (main_b.at[:, g_at], main_s.at[second, g_at]),
        ]
        return [
            pltpu.make_async_copy(source, target, sems.at[c, i])
            for i, (source, target) in enumerate(pairs)
        ]

    for c in range(chunks):
        for copy in copies(c):
            copy.start()
    gate = up = grad = 0.0
    for c in range(chunks):
        at, g_at = pl.ds(c * WIDE, WIDE), pl.ds(width + c * WIDE, WIDE)
        for copy in copies(c):
            copy.wait()
        for i, (exps, turned) in enumerate(((ge, True), (ue, True), (de, False))):
            weights_s[i, :rows, at] = dequantized(codes_s[i, :, at], exps, c, turned)
            weights_s[i, rows:, at] = jnp.zeros((weights_s.shape[1] - rows, WIDE), bf16)
        x = main_s[:, at]
        gate += dot(x, weights_s[0, :, at], 1, 1)
        up += dot(x, weights_s[1, :, at], 1, 1)
        grad += dot(main_s[:, g_at], weights_s[2, :, at], 1, 1)
    grad = imp[...] * grad
    sigma = jax.nn.sigmoid(gate)
    act = gate * sigma
    hid = imp[...] * act * up
    up_delta = grad * act
    gate_delta = grad * up * sigma * (1.0 + gate * (1.0 - sigma))
    for out, value in zip(outs, (hid, gate_delta, up_delta)):
        out[...] = value.T[:rows].astype(bf16)
    gate_delta, up_delta = gate_delta.astype(bf16), up_delta.astype(bf16)
    for c in range(chunks):
        at = pl.ds(c * WIDE, WIDE)
        value = dot(gate_delta, weights_s[0, :, at], 1, 0)
        value += dot(up_delta, weights_s[1, :, at], 1, 0)
        own[:, at] = value[:half].astype(own.dtype)
        send[:, at] = value[half:].astype(send.dtype)


def forward(main_a, main_b, codes, exps, imp, pad):
    half, columns_in = main_a.shape
    hidden, width = codes[0].shape
    tokens = 2 * half
    whole = pl.BlockSpec(memory_space=pl.ANY)
    outs = [((hidden, tokens), bf16)] * 3 + [((half, width), bf16)] * 2
    return pl.pallas_call(
        forward_body,
        grid=(1,),
        in_specs=[whole] * 5
        + [pl.BlockSpec(e.shape, lambda k: (0, 0)) for e in exps]
        + [pl.BlockSpec((tokens, 1), lambda k: (0, 0))],
        out_specs=[pl.BlockSpec(shape, lambda k: (0, 0)) for shape, _ in outs],
        out_shape=[jax.ShapeDtypeStruct(*out) for out in outs],
        scratch_shapes=[
            pltpu.VMEM((tokens, columns_in), bf16),
            pltpu.VMEM((3, hidden, width), bf16),
            pltpu.VMEM((3, pad, width), bf16),
            pltpu.SemaphoreType.DMA((width // WIDE, 7)),
        ],
        compiler_params=params(56),
        cost_estimate=cost(14),
        name="forward",
    )(main_a, main_b, *codes, *exps, imp)


def join_body(*refs):
    pieces, out = refs[:-1], refs[-1]
    row = col = 0
    for piece in pieces:
        rows, cols = piece.shape
        out[row : row + rows, col : col + cols] = piece[...]
        col += cols
        if col == out.shape[1]:
            row, col = row + rows, 0


def join(*layers):
    shape = sum(layer[0].shape[0] for layer in layers), sum(p.shape[1] for p in layers[0])
    pieces = [piece for layer in layers for piece in layer]
    return pl.pallas_call(
        join_body,
        grid=(1,),
        in_specs=[pl.BlockSpec(p.shape, lambda k: (0, 0)) for p in pieces],
        out_specs=pl.BlockSpec(shape, lambda k: (0, 0)),
        out_shape=jax.ShapeDtypeStruct(shape, bf16),
        compiler_params=params(56),
        cost_estimate=cost(3),
        name="join",
    )(*pieces)


def input_body(where, own, received, out):
    out[...] = (own[...].astype(f32) + received[...].astype(f32)).astype(bf16)


def input_sum(where, own, received):
    n, rows, width = own.shape
    block = pl.BlockSpec((1, rows, width), lambda i, w: (i, 0, 0))
    return pl.pallas_call(
        input_body,
        grid_spec=pltpu.PrefetchScalarGridSpec(
            num_scalar_prefetch=1,
            grid=(n,),
            in_specs=[block, block],
            out_specs=pl.BlockSpec((1, rows, width), lambda i, w: (w[i], 0, 0)),
        ),
        out_shape=jax.ShapeDtypeStruct(own.shape, bf16),
        compiler_params=params(16),
        cost_estimate=cost(3),
        name="input_sum",
    )(where, own, received)


def weight_body(where, xa, xb, *refs):
    sides, blocks, (far_a, far_b, send, keep) = refs[:6], refs[6:9], refs[9:]
    rows = jnp.concatenate([r[...] for r in (xa, xb, *sides)], axis=0)
    blocks = [b[...] for b in blocks] + [stack(far_a, far_b)]
    value = dot(jnp.concatenate(blocks, axis=1), rows, 1, 0)
    step, per = pl.program_id(0), pl.num_programs(0) // 2

    @pl.when(step < per)
    def _():
        send[...] = value.astype(bf16)

    @pl.when(step >= per)
    def _():
        keep[...] = value


def weight_part(where, main_a, main_b, side_a, side_b, blocks, second, part):
    half = main_a.shape[0]
    hidden, tokens = blocks[0].shape
    size = 512
    per = part // size

    def spot(first, j, w):
        return (first + w[1 + j // per]) * per + j % per

    group = pl.BlockSpec((half, size), lambda j, w: (0, spot(8 * second + 2 * w[0], j, w)))

    def side(i):
        return pl.BlockSpec((half, size), lambda j, w: (0, spot(4 * i + 2 * second, j, w)))

    return pl.pallas_call(
        weight_body,
        grid_spec=pltpu.PrefetchScalarGridSpec(
            num_scalar_prefetch=1,
            grid=(2 * per,),
            in_specs=[group, group]
            + [side(i) for i in (0, 0, 1, 1, 2, 2)]
            + [pl.BlockSpec(b.shape, lambda j, w: (0, 0)) for b in blocks],
            out_specs=[
                pl.BlockSpec((hidden, size), lambda j, w: (0, jnp.minimum(j, per - 1))),
                pl.BlockSpec((hidden, size), lambda j, w: (0, jnp.maximum(j - per, 0))),
            ],
        ),
        out_shape=[
            jax.ShapeDtypeStruct((hidden, part), bf16),
            jax.ShapeDtypeStruct((hidden, part), f32),
        ],
        compiler_params=params(56),
        cost_estimate=cost(6),
        name="weight_part",
    )(where, main_a, main_b, *[side_a, side_b] * 3, *blocks)


def after(value, earlier):
    return lax.optimization_barrier((value, earlier))[0]


def on_device(
    x_rows,
    out_grad,
    gate_codes,
    gate_exps,
    up_codes,
    up_exps,
    down_codes,
    down_exps,
    replay_slot,
    priorities,
):
    at_x, at_yl = lax.axis_index("x"), lax.axis_index("yl")
    at_z, at_yh, at_core = lax.axis_index("z"), lax.axis_index("yh"), lax.axis_index("core")
    n_x = lax.axis_size("x")
    rows, width = x_rows.shape
    hidden = down_codes.shape[0]
    pad = -(-hidden // LANES) * LANES
    line_part = width // n_x
    part = line_part // lax.axis_size("yl")

    def weigh_tokens(slots):
        total = jnp.sum(priorities)
        importance = lax.rsqrt(priorities.shape[0] * jnp.take(priorities, slots) / total)
        importance = importance.reshape(-1, 2, 2, rows)
        importance = jnp.where(at_yh == 1, importance[:, ::-1], importance)
        importance = jnp.where(at_core == 1, importance[:, :, ::-1], importance)
        importance = jnp.roll(importance, -at_z, axis=0)
        importance = jnp.stack([importance[i] for i in (0, 7, 1, 6, 2, 5, 3, 4)])
        return importance.transpose(2, 0, 1, 3).reshape(-1, 1)

    def both_ways(left, right):
        return shift(left, "z", 1), shift(right, "z", -1)

    together = lax.optimization_barrier

    def cut(blocks):
        group = jnp.stack(blocks).reshape(-1, 2 * width)
        spots = [(at_x + step) % n_x for step in steps]
        return [
            jnp.concatenate(
                [columns(group, spot, line_part), columns(group, spot + n_x, line_part)], axis=1
            )
            for spot in spots
        ]

    def swap_sides(slices):
        return [shift(piece, "x", step) for piece, step in zip(slices, steps)]

    steps = (1, n_x - 1, 2)

    others = shift(x_rows, "yh", 1), shift(out_grad, "yh", 1)
    main = jnp.concatenate(
        [jnp.concatenate([x_rows, out_grad], axis=1), jnp.concatenate(others, axis=1)], axis=0
    )

    ring1 = both_ways(main, main)
    importance = weigh_tokens(after(replay_slot, main))
    ring1, importance = together((ring1, importance))
    ring2 = both_ways(*ring1)
    slices = cut([main, ring1[0]])
    ring2, slices = together((ring2, slices))
    ring3 = both_ways(*ring2)
    sides1 = swap_sides(slices)
    slices = cut([ring1[1], ring2[0]])
    ring3, sides1, slices = together((ring3, sides1, slices))
    split = rows // 8 * 8 + 8
    far = both_ways(ring3[0][:split], ring3[1][split:])
    sides2 = swap_sides(slices)

    far = jnp.concatenate(far, axis=0)
    main_a = jnp.stack([main, *ring1, *ring2, *ring3, far]).reshape(-1, 2 * width)
    main_b = shift(main_a, "core", 1)
    sides3 = swap_sides(cut([ring2[1], *ring3, far]))
    codes, exps = (gate_codes.T, up_codes.T, down_codes), (gate_exps, up_exps, down_exps)
    hid_t, gate_t, up_t, own, send = forward(main_a, main_b, codes, exps, importance, pad)
    hid_t, send, sides2, sides3 = together((hid_t, send, sides2, sides3))

    def along_x(block):
        return shift(block, "x", 1), shift(block, "x", -1)

    def along_x_far(left, right):
        return shift(left[:SPLIT], "x", 1), shift(right[SPLIT:], "x", -1)

    received = shift(send, "core", 1)
    spots = (at_z + jnp.array([0, 7, 1, 6, 2, 5, 3, 4], jnp.int32)) % 8
    own, received = [v.reshape(len(spots), -1, width) for v in (own, received)]
    line = input_sum(spots.astype(jnp.int32), own, received)

    hid_near = along_x(hid_t)
    side_a = join(sides1, sides2, sides3)
    side_b = shift(side_a, "core", 1)
    hid_near, line, side_b = together((hid_near, line, side_b))
    line = lax.all_to_all(line, "z", 0, 0, tiled=True)

    hid_far = along_x_far(*hid_near)
    gate_near = along_x(gate_t)
    hid_far, gate_near = together((hid_far, gate_near))

    where = jnp.stack([at_x, 1 - at_yl, at_yl]).astype(jnp.int32)

    def weight_grad(blocks, second):
        return weight_part(where, main_a, main_b, side_a, side_b, blocks, second, part)

    gate_far = along_x_far(*gate_near)
    up_near = along_x(up_t)
    down = weight_grad((hid_t, *hid_near, *hid_far), 1)
    gate_far, up_near, down = together((gate_far, up_near, down))

    up_far = along_x_far(*up_near)
    down_got = shift(down[0], "yl", 1)
    gate = weight_grad((gate_t, *gate_near, *gate_far), 0)
    up_far, gate = together((up_far, gate))
    gate, down_got = together((gate, down_got))

    gate_got = shift(gate[0], "yl", 1)
    up = weight_grad((up_t, *up_near, *up_far), 0)
    up, gate_got = together((up, gate_got))
    up_got = shift(up[0], "yl", 1)
    line = jnp.sum(after(line, up).astype(f32), axis=0)
    other = shift(line[rows:].astype(bf16), "yh", 1)
    grad_down = (down[1] + down_got.astype(f32)).astype(bf16)
    grad_gate = (gate[1] + gate_got.astype(f32)).astype(bf16).T
    input_grad = (line[:rows] + other.astype(f32)).astype(bf16)
    grad_up = (up[1] + up_got.astype(f32)).astype(bf16).T
    return input_grad, grad_gate, grad_up, grad_down


def solution(mesh):
    fine = Mesh(mesh.devices.reshape(4, 2, 8, 2, 2), ALL)
    return jax.shard_map(
        on_device,
        mesh=fine,
        in_specs=(
            P(ALL, None),
            P(ALL, None),
            P(None, TENSOR),
            P(None, TENSOR),
            P(None, TENSOR),
            P(None, TENSOR),
            P(TENSOR, None),
            P(TENSOR, None),
            P(DP),
            P(),
        ),
        out_specs=(
            P(ALL, None),
            P(DP, TENSOR),
            P(DP, TENSOR),
            P(TENSOR, DP),
        ),
        check_vma=False,
    )
```

```python
import functools

import jax
import jax.numpy as jnp
from jax import lax
from jax.experimental import pallas as pl
from jax.experimental.pallas import tpu as pltpu
from jax.sharding import Mesh, PartitionSpec as P

ALL = ("x", "yl", "z", "yh", "core")
DP = ("x", "yl")
TENSOR = ("z", "yh", "core")
WIDE = 1024
LANES = 128
SPLIT = 240
f32, bf16 = jnp.float32, jnp.bfloat16


def params(mib):
    return pltpu.CompilerParams(vmem_limit_bytes=mib * 2**20)


def cost(us):
    return pl.CostEstimate(flops=2**20, bytes_accessed=int(us * 3e6), transcendentals=0)


def dot(left, right, left_dim, right_dim):
    return lax.dot_general(
        left, right, (((left_dim,), (right_dim,)), ((), ())), preferred_element_type=f32
    )


def stack(first, second):
    return jnp.concatenate([first[...], second[...]], axis=0)


def shift(value, axis, step):
    size = lax.axis_size(axis)
    return lax.ppermute(value, axis, [(i, (i + step) % size) for i in range(size)])


def columns(value, index, width):
    return lax.dynamic_slice_in_dim(value, index * width, width, axis=1)


def dequantized(codes, exps, chunk, turned):
    rows, size = codes.shape
    scale = jnp.exp2(exps[...].astype(f32)).astype(bf16)
    blocks = scale.shape[0 if turned else 1]
    at = lax.broadcasted_iota(jnp.int32, (blocks, size), 1) // LANES + chunk * (size // LANES)
    spread = (at == lax.broadcasted_iota(jnp.int32, (blocks, size), 0)).astype(f32).astype(bf16)
    wide = dot(scale, spread, 0 if turned else 1, 0)
    groups = wide.shape[0]
    wide = jnp.broadcast_to(wide[:, None, :], (groups, rows // groups, size))
    return (codes.astype(f32) * wide.reshape(rows, size)).astype(bf16)


def forward_body(
    main_a, main_b, gate_codes, up_codes, down_codes, ge, ue, de, imp, *refs
):
    outs, (own, send, main_s, codes_s, weights_s, sems) = refs[:3], refs[3:]
    rows, width = gate_codes.shape
    half = main_a.shape[0]
    chunks = width // WIDE

    def copies(c):
        at, g_at = pl.ds(c * WIDE, WIDE), pl.ds(width + c * WIDE, WIDE)
        first, second = pl.ds(0, half), pl.ds(half, half)
        pairs = [
            (gate_codes.at[:, at], codes_s.at[0, :, at]),
            (main_a.at[:, at], main_s.at[first, at]),
            (main_b.at[:, at], main_s.at[second, at]),
            (up_codes.at[:, at], codes_s.at[1, :, at]),
            (down_codes.at[:, at], codes_s.at[2, :, at]),
            (main_a.at[:, g_at], main_s.at[first, g_at]),
            (main_b.at[:, g_at], main_s.at[second, g_at]),
        ]
        return [
            pltpu.make_async_copy(source, target, sems.at[c, i])
            for i, (source, target) in enumerate(pairs)
        ]

    for c in range(chunks):
        for copy in copies(c):
            copy.start()
    gate = up = grad = 0.0
    for c in range(chunks):
        at, g_at = pl.ds(c * WIDE, WIDE), pl.ds(width + c * WIDE, WIDE)
        for copy in copies(c):
            copy.wait()
        for i, (exps, turned) in enumerate(((ge, True), (ue, True), (de, False))):
            weights_s[i, :rows, at] = dequantized(codes_s[i, :, at], exps, c, turned)
            weights_s[i, rows:, at] = jnp.zeros((weights_s.shape[1] - rows, WIDE), bf16)
        x = main_s[:, at]
        gate += dot(x, weights_s[0, :, at], 1, 1)
        up += dot(x, weights_s[1, :, at], 1, 1)
        grad += dot(main_s[:, g_at], weights_s[2, :, at], 1, 1)
    grad = imp[...] * grad
    sigma = jax.nn.sigmoid(gate)
    act = gate * sigma
    hid = imp[...] * act * up
    up_delta = grad * act
    gate_delta = grad * up * sigma * (1.0 + gate * (1.0 - sigma))
    for out, value in zip(outs, (hid, gate_delta, up_delta)):
        out[...] = value.T[:rows].astype(bf16)
    gate_delta, up_delta = gate_delta.astype(bf16), up_delta.astype(bf16)
    for c in range(chunks):
        at = pl.ds(c * WIDE, WIDE)
        value = dot(gate_delta, weights_s[0, :, at], 1, 0)
        value += dot(up_delta, weights_s[1, :, at], 1, 0)
        own[:, at] = value[:half].astype(own.dtype)
        send[:, at] = value[half:].astype(send.dtype)


def forward(main_a, main_b, codes, exps, imp, pad):
    half, columns_in = main_a.shape
    hidden, width = codes[0].shape
    tokens = 2 * half
    whole = pl.BlockSpec(memory_space=pl.ANY)
    outs = [((hidden, tokens), bf16)] * 3 + [((half, width), bf16)] * 2
    return pl.pallas_call(
        forward_body,
        grid=(1,),
        in_specs=[whole] * 5
        + [pl.BlockSpec(e.shape, lambda k: (0, 0)) for e in exps]
        + [pl.BlockSpec((tokens, 1), lambda k: (0, 0))],
        out_specs=[pl.BlockSpec(shape, lambda k: (0, 0)) for shape, _ in outs],
        out_shape=[jax.ShapeDtypeStruct(*out) for out in outs],
        scratch_shapes=[
            pltpu.VMEM((tokens, columns_in), bf16),
            pltpu.VMEM((3, hidden, width), bf16),
            pltpu.VMEM((3, pad, width), bf16),
            pltpu.SemaphoreType.DMA((width // WIDE, 7)),
        ],
        compiler_params=params(44),
        cost_estimate=cost(14),
        name="forward",
    )(main_a, main_b, *codes, *exps, imp)


def join_body(*refs):
    pieces, out = refs[:-1], refs[-1]
    row = col = 0
    for piece in pieces:
        rows, cols = piece.shape
        out[row : row + rows, col : col + cols] = piece[...]
        col += cols
        if col == out.shape[1]:
            row, col = row + rows, 0


def join(*layers):
    shape = sum(layer[0].shape[0] for layer in layers), sum(p.shape[1] for p in layers[0])
    pieces = [piece for layer in layers for piece in layer]
    return pl.pallas_call(
        join_body,
        grid=(1,),
        in_specs=[pl.BlockSpec(p.shape, lambda k: (0, 0)) for p in pieces],
        out_specs=pl.BlockSpec(shape, lambda k: (0, 0)),
        out_shape=jax.ShapeDtypeStruct(shape, bf16),
        compiler_params=params(56),
        cost_estimate=cost(3),
        name="join",
    )(*pieces)


def input_body(where, own, received, out):
    out[...] = (own[...].astype(f32) + received[...].astype(f32)).astype(bf16)


def input_sum(where, own, received):
    n, rows, width = own.shape
    block = pl.BlockSpec((1, rows, width), lambda i, w: (i, 0, 0))
    return pl.pallas_call(
        input_body,
        grid_spec=pltpu.PrefetchScalarGridSpec(
            num_scalar_prefetch=1,
            grid=(n,),
            in_specs=[block, block],
            out_specs=pl.BlockSpec((1, rows, width), lambda i, w: (w[i], 0, 0)),
        ),
        out_shape=jax.ShapeDtypeStruct(own.shape, bf16),
        compiler_params=params(16),
        cost_estimate=cost(3),
        name="input_sum",
    )(where, own, received)


def weight_body(where, xa, xb, *refs):
    sides, blocks, (far_a, far_b, send, keep) = refs[:6], refs[6:9], refs[9:]
    rows = jnp.concatenate([r[...] for r in (xa, xb, *sides)], axis=0)
    blocks = [b[...] for b in blocks] + [stack(far_a, far_b)]
    value = dot(jnp.concatenate(blocks, axis=1), rows, 1, 0)
    step, per = pl.program_id(0), pl.num_programs(0) // 2

    @pl.when(step < per)
    def _():
        send[...] = value.astype(bf16)

    @pl.when(step >= per)
    def _():
        keep[...] = value


def weight_part(where, main_a, main_b, side_a, side_b, blocks, second, part):
    half = main_a.shape[0]
    hidden, tokens = blocks[0].shape
    size = 512
    per = part // size

    def spot(first, j, w):
        return (first + w[1 + j // per]) * per + j % per

    group = pl.BlockSpec((half, size), lambda j, w: (0, spot(8 * second + 2 * w[0], j, w)))

    def side(i):
        return pl.BlockSpec((half, size), lambda j, w: (0, spot(4 * i + 2 * second, j, w)))

    return pl.pallas_call(
        weight_body,
        grid_spec=pltpu.PrefetchScalarGridSpec(
            num_scalar_prefetch=1,
            grid=(2 * per,),
            in_specs=[group, group]
            + [side(i) for i in (0, 0, 1, 1, 2, 2)]
            + [pl.BlockSpec(b.shape, lambda j, w: (0, 0)) for b in blocks],
            out_specs=[
                pl.BlockSpec((hidden, size), lambda j, w: (0, jnp.minimum(j, per - 1))),
                pl.BlockSpec((hidden, size), lambda j, w: (0, jnp.maximum(j - per, 0))),
            ],
        ),
        out_shape=[
            jax.ShapeDtypeStruct((hidden, part), bf16),
            jax.ShapeDtypeStruct((hidden, part), f32),
        ],
        compiler_params=params(56),
        cost_estimate=cost(6),
        name="weight_part",
    )(where, main_a, main_b, *[side_a, side_b] * 3, *blocks)


def after(value, earlier):
    return lax.optimization_barrier((value, earlier))[0]


def on_device(
    x_rows,
    out_grad,
    gate_codes,
    gate_exps,
    up_codes,
    up_exps,
    down_codes,
    down_exps,
    replay_slot,
    priorities,
):
    at_x, at_yl = lax.axis_index("x"), lax.axis_index("yl")
    at_z, at_yh, at_core = lax.axis_index("z"), lax.axis_index("yh"), lax.axis_index("core")
    n_x = lax.axis_size("x")
    rows, width = x_rows.shape
    hidden = down_codes.shape[0]
    pad = -(-hidden // LANES) * LANES
    line_part = width // n_x
    part = line_part // lax.axis_size("yl")

    def weigh_tokens(slots):
        total = jnp.sum(priorities)
        importance = lax.rsqrt(priorities.shape[0] * jnp.take(priorities, slots) / total)
        importance = importance.reshape(-1, 2, 2, rows)
        importance = jnp.where(at_yh == 1, importance[:, ::-1], importance)
        importance = jnp.where(at_core == 1, importance[:, :, ::-1], importance)
        importance = jnp.roll(importance, -at_z, axis=0)
        importance = jnp.stack([importance[i] for i in (0, 7, 1, 6, 2, 5, 3, 4)])
        return importance.transpose(2, 0, 1, 3).reshape(-1, 1)

    def both_ways(left, right):
        return shift(left, "z", 1), shift(right, "z", -1)

    together = lax.optimization_barrier

    def cut(blocks):
        group = jnp.stack(blocks).reshape(-1, 2 * width)
        spots = [(at_x + step) % n_x for step in steps]
        return [
            jnp.concatenate(
                [columns(group, spot, line_part), columns(group, spot + n_x, line_part)], axis=1
            )
            for spot in spots
        ]

    def swap_sides(slices):
        return [shift(piece, "x", step) for piece, step in zip(slices, steps)]

    steps = (1, n_x - 1, 2)

    others = shift(x_rows, "yh", 1), shift(out_grad, "yh", 1)
    main = jnp.concatenate(
        [jnp.concatenate([x_rows, out_grad], axis=1), jnp.concatenate(others, axis=1)], axis=0
    )

    ring1 = both_ways(main, main)
    importance = weigh_tokens(after(replay_slot, main))
    ring1, importance = together((ring1, importance))
    ring2 = both_ways(*ring1)
    slices = cut([main, ring1[0]])
    ring2, slices = together((ring2, slices))
    ring3 = both_ways(*ring2)
    sides1 = swap_sides(slices)
    slices = cut([ring1[1], ring2[0]])
    ring3, sides1, slices = together((ring3, sides1, slices))
    split = rows // 8 * 8 + 8
    far = both_ways(ring3[0][:split], ring3[1][split:])
    sides2 = swap_sides(slices)

    far = jnp.concatenate(far, axis=0)
    main_a = jnp.stack([main, *ring1, *ring2, *ring3, far]).reshape(-1, 2 * width)
    main_b = shift(main_a, "core", 1)
    sides3 = swap_sides(cut([ring2[1], *ring3, far]))
    codes, exps = (gate_codes.T, up_codes.T, down_codes), (gate_exps, up_exps, down_exps)
    hid_t, gate_t, up_t, own, send = forward(main_a, main_b, codes, exps, importance, pad)
    hid_t, send, sides2 = together((hid_t, send, sides2))

    def along_x(block):
        return shift(block, "x", 1), shift(block, "x", -1)

    def along_x_far(left, right):
        return shift(left[:SPLIT], "x", 1), shift(right[SPLIT:], "x", -1)

    received = shift(send, "core", 1)
    spots = (at_z + jnp.array([0, 7, 1, 6, 2, 5, 3, 4], jnp.int32)) % 8
    own, received = [v.reshape(len(spots), -1, width) for v in (own, received)]
    line = input_sum(spots.astype(jnp.int32), own, received)

    hid_near = along_x(hid_t)
    side_a = join(sides1, sides2, sides3)
    side_b = shift(side_a, "core", 1)
    hid_near, line = together((hid_near, line))
    line = lax.all_to_all(line, "z", 0, 0, tiled=True)

    hid_far = along_x_far(*hid_near)
    gate_near = along_x(gate_t)
    hid_far, gate_near, side_b = together((hid_far, gate_near, side_b))

    where = jnp.stack([at_x, 1 - at_yl, at_yl]).astype(jnp.int32)

    def weight_grad(blocks, second):
        return weight_part(where, main_a, main_b, side_a, side_b, blocks, second, part)

    gate_far = along_x_far(*gate_near)
    up_near = along_x(up_t)
    down = weight_grad((hid_t, *hid_near, *hid_far), 1)
    gate_far, up_near, down = together((gate_far, up_near, down))

    up_far = along_x_far(*up_near)
    down_got = shift(down[0], "yl", 1)
    gate = weight_grad((gate_t, *gate_near, *gate_far), 0)
    up_far, gate = together((up_far, gate))
    gate, down_got = together((gate, down_got))

    gate_got = shift(gate[0], "yl", 1)
    up = weight_grad((up_t, *up_near, *up_far), 0)
    up, gate_got = together((up, gate_got))
    up_got = shift(up[0], "yl", 1)
    line = jnp.sum(after(line, up).astype(f32), axis=0)
    other = shift(line[rows:].astype(bf16), "yh", 1)
    grad_down = (down[1] + down_got.astype(f32)).astype(bf16)
    grad_gate = (gate[1] + gate_got.astype(f32)).astype(bf16).T
    input_grad = (line[:rows] + other.astype(f32)).astype(bf16)
    grad_up = (up[1] + up_got.astype(f32)).astype(bf16).T
    return input_grad, grad_gate, grad_up, grad_down


def solution(mesh):
    fine = Mesh(mesh.devices.reshape(4, 2, 8, 2, 2), ALL)
    return jax.shard_map(
        on_device,
        mesh=fine,
        in_specs=(
            P(ALL, None),
            P(ALL, None),
            P(None, TENSOR),
            P(None, TENSOR),
            P(None, TENSOR),
            P(None, TENSOR),
            P(TENSOR, None),
            P(TENSOR, None),
            P(DP),
            P(),
        ),
        out_specs=(
            P(ALL, None),
            P(DP, TENSOR),
            P(DP, TENSOR),
            P(TENSOR, DP),
        ),
        check_vma=False,
    )
```

```python
import functools

import jax
import jax.numpy as jnp
from jax import lax
from jax.experimental import pallas as pl
from jax.experimental.pallas import tpu as pltpu
from jax.sharding import Mesh, PartitionSpec as P

ALL = ("x", "yl", "z", "yh", "core")
DP = ("x", "yl")
TENSOR = ("z", "yh", "core")
WIDE = 1024
LANES = 128
SPLIT = 240
f32, bf16 = jnp.float32, jnp.bfloat16


def params(mib):
    return pltpu.CompilerParams(vmem_limit_bytes=mib * 2**20)


def cost(us):
    return pl.CostEstimate(flops=2**20, bytes_accessed=int(us * 3e6), transcendentals=0)


def dot(left, right, left_dim, right_dim):
    return lax.dot_general(
        left, right, (((left_dim,), (right_dim,)), ((), ())), preferred_element_type=f32
    )


def stack(first, second):
    return jnp.concatenate([first[...], second[...]], axis=0)


def shift(value, axis, step):
    size = lax.axis_size(axis)
    return lax.ppermute(value, axis, [(i, (i + step) % size) for i in range(size)])


def columns(value, index, width):
    return lax.dynamic_slice_in_dim(value, index * width, width, axis=1)


def dequantized(codes, exps, chunk, turned):
    rows, size = codes.shape
    scale = jnp.exp2(exps[...].astype(f32)).astype(bf16)
    blocks = scale.shape[0 if turned else 1]
    at = lax.broadcasted_iota(jnp.int32, (blocks, size), 1) // LANES + chunk * (size // LANES)
    spread = (at == lax.broadcasted_iota(jnp.int32, (blocks, size), 0)).astype(f32).astype(bf16)
    wide = dot(scale, spread, 0 if turned else 1, 0)
    groups = wide.shape[0]
    wide = jnp.broadcast_to(wide[:, None, :], (groups, rows // groups, size))
    return (codes.astype(f32) * wide.reshape(rows, size)).astype(bf16)


def forward_body(
    main_a, main_b, gate_codes, up_codes, down_codes, ge, ue, de, imp, *refs
):
    outs, (own, send, main_s, codes_s, weights_s, sems) = refs[:3], refs[3:]
    rows, width = gate_codes.shape
    half = main_a.shape[0]
    chunks = width // WIDE

    def copies(c):
        at, g_at = pl.ds(c * WIDE, WIDE), pl.ds(width + c * WIDE, WIDE)
        first, second = pl.ds(0, half), pl.ds(half, half)
        pairs = [
            (gate_codes.at[:, at], codes_s.at[0, :, at]),
            (main_a.at[:, at], main_s.at[first, at]),
            (main_b.at[:, at], main_s.at[second, at]),
            (up_codes.at[:, at], codes_s.at[1, :, at]),
            (down_codes.at[:, at], codes_s.at[2, :, at]),
            (main_a.at[:, g_at], main_s.at[first, g_at]),
            (main_b.at[:, g_at], main_s.at[second, g_at]),
        ]
        return [
            pltpu.make_async_copy(source, target, sems.at[c, i])
            for i, (source, target) in enumerate(pairs)
        ]

    for c in range(chunks):
        for copy in copies(c):
            copy.start()
    gate = up = grad = 0.0
    for c in range(chunks):
        at, g_at = pl.ds(c * WIDE, WIDE), pl.ds(width + c * WIDE, WIDE)
        for copy in copies(c):
            copy.wait()
        for i, (exps, turned) in enumerate(((ge, True), (ue, True), (de, False))):
            weights_s[i, :rows, at] = dequantized(codes_s[i, :, at], exps, c, turned)
            weights_s[i, rows:, at] = jnp.zeros((weights_s.shape[1] - rows, WIDE), bf16)
        x = main_s[:, at]
        gate += dot(x, weights_s[0, :, at], 1, 1)
        up += dot(x, weights_s[1, :, at], 1, 1)
        grad += dot(main_s[:, g_at], weights_s[2, :, at], 1, 1)
    grad = imp[...] * grad
    sigma = jax.nn.sigmoid(gate)
    act = gate * sigma
    hid = imp[...] * act * up
    up_delta = grad * act
    gate_delta = grad * up * sigma * (1.0 + gate * (1.0 - sigma))
    for out, value in zip(outs, (hid, gate_delta, up_delta)):
        out[...] = value.T[:rows].astype(bf16)
    gate_delta, up_delta = gate_delta.astype(bf16), up_delta.astype(bf16)
    for c in range(chunks):
        at = pl.ds(c * WIDE, WIDE)
        value = dot(gate_delta, weights_s[0, :, at], 1, 0)
        value += dot(up_delta, weights_s[1, :, at], 1, 0)
        own[:, at] = value[:half].astype(own.dtype)
        send[:, at] = value[half:].astype(send.dtype)


def forward(main_a, main_b, codes, exps, imp, pad):
    half, columns_in = main_a.shape
    hidden, width = codes[0].shape
    tokens = 2 * half
    whole = pl.BlockSpec(memory_space=pl.ANY)
    outs = [((hidden, tokens), bf16)] * 3 + [((half, width), bf16)] * 2
    return pl.pallas_call(
        forward_body,
        grid=(1,),
        in_specs=[whole] * 5
        + [pl.BlockSpec(e.shape, lambda k: (0, 0)) for e in exps]
        + [pl.BlockSpec((tokens, 1), lambda k: (0, 0))],
        out_specs=[pl.BlockSpec(shape, lambda k: (0, 0)) for shape, _ in outs],
        out_shape=[jax.ShapeDtypeStruct(*out) for out in outs],
        scratch_shapes=[
            pltpu.VMEM((tokens, columns_in), bf16),
            pltpu.VMEM((3, hidden, width), bf16),
            pltpu.VMEM((3, pad, width), bf16),
            pltpu.SemaphoreType.DMA((width // WIDE, 7)),
        ],
        compiler_params=params(44),
        cost_estimate=cost(14),
        name="forward",
    )(main_a, main_b, *codes, *exps, imp)


def join_body(*refs):
    pieces, out = refs[:-1], refs[-1]
    row = col = 0
    for piece in pieces:
        rows, cols = piece.shape
        out[row : row + rows, col : col + cols] = piece[...]
        col += cols
        if col == out.shape[1]:
            row, col = row + rows, 0


def join(*layers):
    shape = sum(layer[0].shape[0] for layer in layers), sum(p.shape[1] for p in layers[0])
    pieces = [piece for layer in layers for piece in layer]
    return pl.pallas_call(
        join_body,
        grid=(1,),
        in_specs=[pl.BlockSpec(p.shape, lambda k: (0, 0)) for p in pieces],
        out_specs=pl.BlockSpec(shape, lambda k: (0, 0)),
        out_shape=jax.ShapeDtypeStruct(shape, bf16),
        compiler_params=params(16),
        cost_estimate=cost(3),
        name="join",
    )(*pieces)


def input_body(where, own, received, out):
    out[...] = (own[...].astype(f32) + received[...].astype(f32)).astype(bf16)


def input_sum(where, own, received):
    n, rows, width = own.shape
    block = pl.BlockSpec((1, rows, width), lambda i, w: (i, 0, 0))
    return pl.pallas_call(
        input_body,
        grid_spec=pltpu.PrefetchScalarGridSpec(
            num_scalar_prefetch=1,
            grid=(n,),
            in_specs=[block, block],
            out_specs=pl.BlockSpec((1, rows, width), lambda i, w: (w[i], 0, 0)),
        ),
        out_shape=jax.ShapeDtypeStruct(own.shape, bf16),
        compiler_params=params(16),
        cost_estimate=cost(3),
        name="input_sum",
    )(where, own, received)


def weight_body(where, xa, xb, *refs):
    sides, blocks, (far_a, far_b, send, keep) = refs[:6], refs[6:9], refs[9:]
    rows = jnp.concatenate([r[...] for r in (xa, xb, *sides)], axis=0)
    blocks = [b[...] for b in blocks] + [stack(far_a, far_b)]
    value = dot(jnp.concatenate(blocks, axis=1), rows, 1, 0)
    step, per = pl.program_id(0), pl.num_programs(0) // 2

    @pl.when(step < per)
    def _():
        send[...] = value.astype(bf16)

    @pl.when(step >= per)
    def _():
        keep[...] = value


def weight_part(where, main_a, main_b, side_a, side_b, blocks, second, part):
    half = main_a.shape[0]
    hidden, tokens = blocks[0].shape
    size = 512
    per = part // size

    def spot(first, j, w):
        return (first + w[1 + j // per]) * per + j % per

    group = pl.BlockSpec((half, size), lambda j, w: (0, spot(8 * second + 2 * w[0], j, w)))

    def side(i):
        return pl.BlockSpec((half, size), lambda j, w: (0, spot(4 * i + 2 * second, j, w)))

    return pl.pallas_call(
        weight_body,
        grid_spec=pltpu.PrefetchScalarGridSpec(
            num_scalar_prefetch=1,
            grid=(2 * per,),
            in_specs=[group, group]
            + [side(i) for i in (0, 0, 1, 1, 2, 2)]
            + [pl.BlockSpec(b.shape, lambda j, w: (0, 0)) for b in blocks],
            out_specs=[
                pl.BlockSpec((hidden, size), lambda j, w: (0, jnp.minimum(j, per - 1))),
                pl.BlockSpec((hidden, size), lambda j, w: (0, jnp.maximum(j - per, 0))),
            ],
        ),
        out_shape=[
            jax.ShapeDtypeStruct((hidden, part), bf16),
            jax.ShapeDtypeStruct((hidden, part), f32),
        ],
        compiler_params=params(56),
        cost_estimate=cost(6),
        name="weight_part",
    )(where, main_a, main_b, *[side_a, side_b] * 3, *blocks)


def after(value, earlier):
    return lax.optimization_barrier((value, earlier))[0]


def on_device(
    x_rows,
    out_grad,
    gate_codes,
    gate_exps,
    up_codes,
    up_exps,
    down_codes,
    down_exps,
    replay_slot,
    priorities,
):
    at_x, at_yl = lax.axis_index("x"), lax.axis_index("yl")
    at_z, at_yh, at_core = lax.axis_index("z"), lax.axis_index("yh"), lax.axis_index("core")
    n_x = lax.axis_size("x")
    rows, width = x_rows.shape
    hidden = down_codes.shape[0]
    pad = -(-hidden // LANES) * LANES
    line_part = width // n_x
    part = line_part // lax.axis_size("yl")

    def weigh_tokens(slots):
        total = jnp.sum(priorities)
        importance = lax.rsqrt(priorities.shape[0] * jnp.take(priorities, slots) / total)
        importance = importance.reshape(-1, 2, 2, rows)
        importance = jnp.where(at_yh == 1, importance[:, ::-1], importance)
        importance = jnp.where(at_core == 1, importance[:, :, ::-1], importance)
        importance = jnp.roll(importance, -at_z, axis=0)
        importance = jnp.stack([importance[i] for i in (0, 7, 1, 6, 2, 5, 3, 4)])
        return importance.transpose(2, 0, 1, 3).reshape(-1, 1)

    def both_ways(left, right):
        return shift(left, "z", 1), shift(right, "z", -1)

    together = lax.optimization_barrier

    def cut(blocks):
        group = jnp.stack(blocks).reshape(-1, 2 * width)
        spots = [(at_x + step) % n_x for step in steps]
        return [
            jnp.concatenate(
                [columns(group, spot, line_part), columns(group, spot + n_x, line_part)], axis=1
            )
            for spot in spots
        ]

    def swap_sides(slices):
        return [shift(piece, "x", step) for piece, step in zip(slices, steps)]

    steps = (1, n_x - 1, 2)

    others = shift(x_rows, "yh", 1), shift(out_grad, "yh", 1)
    main = jnp.concatenate(
        [jnp.concatenate([x_rows, out_grad], axis=1), jnp.concatenate(others, axis=1)], axis=0
    )

    ring1 = both_ways(main, main)
    importance = weigh_tokens(after(replay_slot, main))
    ring1, importance = together((ring1, importance))
    ring2 = both_ways(*ring1)
    slices = cut([main, ring1[0]])
    ring2, slices = together((ring2, slices))
    ring3 = both_ways(*ring2)
    sides1 = swap_sides(slices)
    slices = cut([ring1[1], ring2[0]])
    ring3, sides1, slices = together((ring3, sides1, slices))
    split = rows // 8 * 8 + 8
    far = both_ways(ring3[0][:split], ring3[1][split:])
    sides2 = swap_sides(slices)

    far = jnp.concatenate(far, axis=0)
    main_a = jnp.stack([main, *ring1, *ring2, *ring3, far]).reshape(-1, 2 * width)
    main_b = shift(main_a, "core", 1)
    sides3 = swap_sides(cut([ring2[1], *ring3, far]))
    codes, exps = (gate_codes.T, up_codes.T, down_codes), (gate_exps, up_exps, down_exps)
    hid_t, gate_t, up_t, own, send = forward(main_a, main_b, codes, exps, importance, pad)
    hid_t, send, sides2 = together((hid_t, send, sides2))

    def along_x(block):
        return shift(block, "x", 1), shift(block, "x", -1)

    def along_x_far(left, right):
        return shift(left[:SPLIT], "x", 1), shift(right[SPLIT:], "x", -1)

    received = shift(send, "core", 1)
    spots = (at_z + jnp.array([0, 7, 1, 6, 2, 5, 3, 4], jnp.int32)) % 8
    own, received = [v.reshape(len(spots), -1, width) for v in (own, received)]
    line = input_sum(spots.astype(jnp.int32), own, received)

    hid_near = along_x(hid_t)
    side_a = join(sides1, sides2, sides3)
    side_b = shift(side_a, "core", 1)
    hid_near, line = together((hid_near, line))
    line = lax.all_to_all(line, "z", 0, 0, tiled=True)

    hid_far = along_x_far(*hid_near)
    gate_near = along_x(gate_t)
    hid_far, gate_near, side_b = together((hid_far, gate_near, side_b))

    where = jnp.stack([at_x, 1 - at_yl, at_yl]).astype(jnp.int32)

    def weight_grad(blocks, second):
        return weight_part(where, main_a, main_b, side_a, side_b, blocks, second, part)

    gate_far = along_x_far(*gate_near)
    up_near = along_x(up_t)
    down = weight_grad((hid_t, *hid_near, *hid_far), 1)
    gate_far, up_near, down = together((gate_far, up_near, down))

    up_far = along_x_far(*up_near)
    down_got = shift(down[0], "yl", 1)
    gate = weight_grad((gate_t, *gate_near, *gate_far), 0)
    up_far, gate = together((up_far, gate))
    gate, down_got = together((gate, down_got))

    gate_got = shift(gate[0], "yl", 1)
    up = weight_grad((up_t, *up_near, *up_far), 0)
    up, gate_got = together((up, gate_got))
    up_got = shift(up[0], "yl", 1)
    line = jnp.sum(after(line, up).astype(f32), axis=0)
    other = shift(line[rows:].astype(bf16), "yh", 1)
    grad_down = (down[1] + down_got.astype(f32)).astype(bf16)
    grad_gate = (gate[1] + gate_got.astype(f32)).astype(bf16).T
    input_grad = (line[:rows] + other.astype(f32)).astype(bf16)
    grad_up = (up[1] + up_got.astype(f32)).astype(bf16).T
    return input_grad, grad_gate, grad_up, grad_down


def solution(mesh):
    fine = Mesh(mesh.devices.reshape(4, 2, 8, 2, 2), ALL)
    return jax.shard_map(
        on_device,
        mesh=fine,
        in_specs=(
            P(ALL, None),
            P(ALL, None),
            P(None, TENSOR),
            P(None, TENSOR),
            P(None, TENSOR),
            P(None, TENSOR),
            P(TENSOR, None),
            P(TENSOR, None),
            P(DP),
            P(),
        ),
        out_specs=(
            P(ALL, None),
            P(DP, TENSOR),
            P(DP, TENSOR),
            P(TENSOR, DP),
        ),
        check_vma=False,
    )
```
